32 devices in a mesh: row: 4 (over x, core), col: 8 (over z, y).
Axes of the slice: x: 2, y: 2, z: 4, core: 2. Of those that a mesh axis runs over, the one named last changes fastest.
Arguments:
- object_field: float32 [2, 2048, 4096], P(None, 'row', 'col'), may hold values from -5 to 5
- probe: float32 [2, 256, 256], replicated, may hold values from -5 to 5
- amplitude: float32 [4, 8, 8, 256, 256], P('row', 'col'), may hold values from 0.2 to 3
- offsets: int32 [4, 8, 8, 2], P('row', 'col'), may hold values from 0 to 511
Outputs:
- object_grad: float32 [2, 2048, 4096], P(None, 'row', 'col')
- probe_grad: float32 [2, 256, 256], replicated
The draws below stay inside these ranges and needn't reach their ends.
All inputs are finite; a program needn't handle non-finite values.
Results may differ from the reference program's by a relative error of at most 0.0003.
Values sent between devices are 32-bit elements; how exact they have to be, the bound alone decides.
A program may use at most 64 MiB of HBM per device.

```python
import math
import jax
import jax.numpy as jnp
from jax import lax

PS = 256
TILE = 512
PATCHES = 8
GRID_R = 4
GRID_C = 8
NR = 2048
NC = 4096


def with_ends(entries, rng, least, top_value):
    extent = entries.shape
    index_at = [jax.random.randint(jax.random.fold_in(rng, axis), (), 0, extent[axis]) for axis in range(len(extent))]
    entries = entries.at[tuple(index_at)].set(least)
    longest = extent.index(max(extent))
    index_at[longest] = (index_at[longest] + 1) % extent[longest]
    return entries.at[tuple(index_at)].set(top_value)


def levels(own_key, extent, shards, low, top_value):
    loudness, own = 1.0, jax.random.fold_in(own_key, 6)
    for axis_at, shards_of in shards:
        draws = jnp.exp(jax.random.uniform(jax.random.fold_in(own, axis_at), (shards_of,), jnp.float32, low / len(shards), top_value / len(shards)))
        loudness = loudness * jnp.repeat(draws, extent[axis_at] // shards_of).reshape([-1 if axis == axis_at else 1 for axis in range(len(extent))])
    return loudness


def noise(rng, dims, width, reach, shards=(), kind=jnp.bfloat16):
    array = jax.random.normal(rng, dims, jnp.float32) * width
    if len(shards) > 0:
        array = levels(rng, dims, shards, -0.22, 0.18) * array
    return jnp.clip(array, min=-reach, max=reach).astype(kind)


def setup_inputs(seed: int = 0) -> dict:
    splits = jax.random.split(jax.random.key(seed), 5)
    object_field = noise(splits[0], (2, NR, NC), 0.7, 5.0, ((1, 4), (2, 8)), jnp.float32)
    probe = noise(splits[1], (2, PS, PS), 0.7, 5.0, (), jnp.float32)
    amplitude = jnp.clip(jnp.exp(math.log(3.0) - 2.7080502 * jax.random.uniform(splits[2], (GRID_R, GRID_C, PATCHES, PS, PS), jnp.float32) ** levels(splits[2], (GRID_R, GRID_C, PATCHES, PS, PS), ((0, 4), (1, 8)), -0.2, 0.2)), 0.2, 3.0)
    offsets = with_ends(jax.random.randint(splits[3], (GRID_R, GRID_C, PATCHES, 2), 0, TILE), jax.random.fold_in(splits[3], 1), 0, TILE - 1).astype(jnp.int32)
    return dict(object_field=object_field, probe=probe, amplitude=amplitude, offsets=offsets)


def tables(size):
    index = jnp.arange(size, dtype=jnp.int32)
    product = index[:, None] * index[None, :] % size
    angle = product.astype(jnp.float32) * (2.0 * math.pi / size)
    scale = 1.0 / math.sqrt(size)
    return (jnp.cos(angle) * scale, jnp.sin(angle) * scale)

def matmul(left, right):
    return jnp.dot(left, right, precision=lax.Precision.HIGHEST, preferred_element_type=jnp.float32)

def transform(real_part, imag_part, cosine, sine, sign):
    left_r = matmul(cosine, real_part) - sign * matmul(sine, imag_part)
    left_i = matmul(cosine, imag_part) + sign * matmul(sine, real_part)
    out_r = matmul(left_r, cosine) - sign * matmul(left_i, sine)
    out_i = matmul(left_i, cosine) + sign * matmul(left_r, sine)
    return (out_r, out_i)

def patch_terms(view, probe, amp, cosine, sine):
    probe_r, probe_i = (probe[0], probe[1])
    view_r, view_i = (view[0], view[1])
    wave_r = probe_r * view_r - probe_i * view_i
    wave_i = probe_r * view_i + probe_i * view_r
    far_r, far_i = transform(wave_r, wave_i, cosine, sine, -1.0)
    modulus = jnp.sqrt(far_r * far_r + far_i * far_i)
    keep = 1.0 - amp / jnp.maximum(modulus, 0.5)
    chi_r, chi_i = transform(far_r * keep, far_i * keep, cosine, sine, 1.0)
    obj_term = jnp.stack([probe_r * chi_r + probe_i * chi_i, probe_r * chi_i - probe_i * chi_r])
    probe_term = jnp.stack([view_r * chi_r + view_i * chi_i, view_r * chi_i - view_i * chi_r])
    return (obj_term, probe_term)

def reference(object_field, probe, amplitude, offsets):
    cosine, sine = tables(PS)
    padded = jnp.pad(object_field, ((0, 0), (0, PS), (0, PS)))
    flat_off = offsets.reshape(-1, 2).astype(jnp.int32)
    flat_amp = amplitude.reshape(-1, PS, PS)
    count = GRID_R * GRID_C * PATCHES
    numbers = jnp.arange(count, dtype=jnp.int32)

    def step(carry, item):
        grad, probe_acc = carry
        number, off, amp = item
        tile_r = number // (GRID_C * PATCHES)
        tile_c = number // PATCHES % GRID_C
        top = (tile_r * TILE + off[0]).astype(jnp.int32)
        left = (tile_c * TILE + off[1]).astype(jnp.int32)
        zero = jnp.zeros((), jnp.int32)
        view = lax.dynamic_slice(padded, (zero, top, left), (2, PS, PS))
        obj_term, probe_term = patch_terms(view, probe, amp, cosine, sine)
        old = lax.dynamic_slice(grad, (zero, top, left), (2, PS, PS))
        grad = lax.dynamic_update_slice(grad, old + obj_term, (zero, top, left))
        return ((grad, probe_acc + probe_term), None)
    start = (jnp.zeros(padded.shape, jnp.float32), jnp.zeros((2, PS, PS), jnp.float32))
    (grad, probe_acc), _ = lax.scan(step, start, (numbers, flat_off, flat_amp))
    return (grad[:, :NR, :NC], probe_acc / count)
```

```python
import functools
import math

import jax
import jax.numpy as jnp
import ml_dtypes
import numpy as np
from jax import lax
from jax.experimental import pallas as pl
from jax.experimental.pallas import tpu as pltpu
from jax.sharding import PartitionSpec as P

LANES = 128
SUBLANES = 8
GROUP = 2


def passed_along(value, axis, steps):
    count = lax.axis_size(axis)
    first, last = (max(0, -steps), min(count, count - steps))
    return lax.ppermute(value, axis, [(source, source + steps) for source in range(first, last)])


def halves_np(table):
    high = table.astype(ml_dtypes.bfloat16)
    low = (table - high.astype(np.float64)).astype(ml_dtypes.bfloat16)
    return high, low


def tables(size):
    index = np.arange(size)
    angle = (index[:, None] * index[None, :] % size) * (2.0 * math.pi / size)
    cosine, sine = np.cos(angle) / math.sqrt(size), np.sin(angle) / math.sqrt(size)
    left, right = [], []
    for table in (cosine, sine - cosine, cosine + sine):
        high, low = halves_np(table)
        left.append(np.concatenate([high, high, low], axis=1))
        right.append(np.concatenate([high, low, high], axis=0))
    return np.stack(left), np.stack(right)


def halves(value):
    high = value.astype(jnp.bfloat16)
    return high, (value - high.astype(jnp.float32)).astype(jnp.bfloat16)


def from_left(table, value):
    high, low = halves(value)
    return jnp.dot(table, jnp.concatenate([high, low, high], axis=0), preferred_element_type=jnp.float32)


def from_right(table, value):
    high, low = halves(value)
    return jnp.dot(jnp.concatenate([high, high, low], axis=1), table, preferred_element_type=jnp.float32)


def transform(real, imag, left, right, forward):
    for product, table in ((from_left, left), (from_right, right)):
        shared = product(table[0], real + imag)
        if forward:
            real, imag = shared + product(table[1], imag), shared - product(table[2], real)
        else:
            real, imag = shared - product(table[2], imag), shared + product(table[1], real)
    return real, imag


def kernel(dims, off, obj, below, right_top, right_low, corner, probe, amp, left_t, right_t,
           g_main, g_below, g_right_top, g_right_low, g_corner, probe_acc, ext, grad, sems):
    side, rows, cols = dims
    step = pl.program_id(0)

    def pieces(buf):
        return (
            buf.at[:, pl.ds(0, rows), pl.ds(0, cols)],
            buf.at[:, pl.ds(rows, side), pl.ds(0, cols)],
            buf.at[:, pl.ds(0, side), pl.ds(cols, side)],
            buf.at[:, pl.ds(side, rows - side), pl.ds(cols, side)],
            buf.at[:, pl.ds(rows, side), pl.ds(cols, side)],
        )

    @pl.when(step == 0)
    def _():
        copies = [
            pltpu.make_async_copy(source, place, sems.at[number])
            for number, (source, place) in enumerate(
                zip((obj, below, right_top, right_low, corner), pieces(ext))
            )
        ]
        for copy in copies:
            copy.start()
        grad[...] = jnp.zeros_like(grad)
        probe_acc[...] = jnp.zeros_like(probe_acc)
        for copy in copies:
            copy.wait()

    wide, tall = side + LANES, side + SUBLANES
    probe_r, probe_i = probe[0], probe[1]
    found = []
    for item in range(GROUP):
        top = off[0, 0, step * GROUP + item, 0]
        at = off[0, 0, step * GROUP + item, 1]
        base = pl.multiple_of(at // LANES * LANES, LANES)
        shift = at - base
        start = pl.multiple_of(top // SUBLANES * SUBLANES, SUBLANES)
        drop = top - start

        def view_of(part):
            window = ext[part, pl.ds(start, tall), pl.ds(base, wide)]
            window = pltpu.roll(window, lax.rem(wide - shift, wide), 1)[:, :side]
            return pltpu.roll(window, lax.rem(tall - drop, tall), 0)[:side]

        view_r, view_i = view_of(0), view_of(1)
        wave_r = probe_r * view_r - probe_i * view_i
        wave_i = probe_r * view_i + probe_i * view_r
        far_r, far_i = transform(wave_r, wave_i, left_t, right_t, True)
        keep = 1.0 - amp[item] * lax.rsqrt(jnp.maximum(far_r * far_r + far_i * far_i, 0.25))
        chi_r, chi_i = transform(far_r * keep, far_i * keep, left_t, right_t, False)
        found.append((start, drop, base, shift, view_r, view_i, chi_r, chi_i))
    for start, drop, base, shift, view_r, view_i, chi_r, chi_i in found:
        terms = (probe_r * chi_r + probe_i * chi_i, probe_r * chi_i - probe_i * chi_r)
        for part in range(2):
            term = jnp.concatenate([terms[part], jnp.zeros((SUBLANES, side), jnp.float32)], axis=0)
            term = pltpu.roll(term, drop, 0)
            term = jnp.concatenate([term, jnp.zeros((tall, LANES), jnp.float32)], axis=1)
            grad[part, pl.ds(start, tall), pl.ds(base, wide)] += pltpu.roll(term, shift, 1)
        probe_acc[0] += view_r * chi_r + view_i * chi_i
        probe_acc[1] += view_r * chi_i - view_i * chi_r

    @pl.when(step == pl.num_programs(0) - 1)
    def _():
        copies = [
            pltpu.make_async_copy(place, target, sems.at[number])
            for number, (place, target) in enumerate(
                zip(pieces(grad), (g_main, g_below, g_right_top, g_right_low, g_corner))
            )
        ]
        for copy in copies:
            copy.start()
        for copy in copies:
            copy.wait()


def all_positions(offsets, obj, below, right_top, right_low, corner, probe, amp):
    side, rows, cols = probe.shape[1], obj.shape[1], obj.shape[2]
    count = offsets.shape[2]
    left_t, right_t = tables(side)
    anywhere = pl.BlockSpec(memory_space=pl.ANY)
    whole = lambda *shape: pl.BlockSpec(shape, lambda step: (0,) * len(shape))
    f32 = jnp.float32
    shape = lambda *dims: jax.ShapeDtypeStruct(dims, f32)
    return pl.pallas_call(
        functools.partial(kernel, (side, rows, cols)),
        grid=(count // GROUP,),
        in_specs=[pl.BlockSpec(memory_space=pltpu.SMEM)] + [anywhere] * 5 + [
            whole(2, side, side),
            pl.BlockSpec((GROUP, side, side), lambda step: (step, 0, 0)),
            whole(*left_t.shape),
            whole(*right_t.shape),
        ],
        out_specs=[anywhere] * 5 + [whole(2, side, side)],
        out_shape=[
            shape(2, rows, cols),
            shape(2, side, cols),
            shape(2, side, side),
            shape(2, rows - side, side),
            shape(2, side, side),
            shape(2, side, side),
        ],
        scratch_shapes=[
            pltpu.VMEM((2, rows + side, cols + side), f32),
            pltpu.VMEM((2, rows + side, cols + side), f32),
            pltpu.SemaphoreType.DMA((5,)),
        ],
        compiler_params=pltpu.CompilerParams(vmem_limit_bytes=44 * 2**20),
        cost_estimate=pl.CostEstimate(
            flops=count * 36 * 2 * side**3, bytes_accessed=12 * 2**20, transcendentals=0
        ),
    )(offsets, obj, below, right_top, right_low, corner, probe, amp,
      jnp.asarray(left_t), jnp.asarray(right_t))


def shards(object_field, probe, amplitude, offsets):
    rows, cols = object_field.shape[1:]
    side = probe.shape[1]
    positions = offsets.shape[2]
    right_top = passed_along(object_field[:, :side, :side], "col", -1)
    right_low = passed_along(object_field[:, side:, :side], "col", -1)
    below = passed_along(object_field[:, :side, :], "row", -1)
    corner = passed_along(right_top, "row", -1)
    g_main, g_below, g_top, g_low, g_corner, probe_acc = all_positions(
        offsets, object_field, below, right_top, right_low, corner, probe,
        amplitude.reshape(amplitude.shape[2:]),
    )
    got_corner = passed_along(g_corner, "row", 1)
    got_low = passed_along(g_low, "col", 1)
    got_rows = passed_along(g_below, "row", 1)
    got_top = passed_along(g_top + got_corner, "col", 1)
    pad = lambda value, top: jnp.pad(
        value, ((0, 0), (top, rows - top - value.shape[1]), (0, cols - value.shape[2]))
    )
    object_grad = g_main + pad(got_rows, 0) + pad(got_top, 0) + pad(got_low, side)
    count = positions * lax.axis_size("row") * lax.axis_size("col")
    probe_total = lax.psum(probe_acc, ("row", "col"))
    return (object_grad, probe_total / count)


def solution(mesh):
    placed = (
        P(None, "row", "col"),
        P(),
        P("row", "col", None, None, None),
        P("row", "col", None, None),
    )
    return jax.shard_map(
        shards, mesh=mesh, in_specs=placed, out_specs=(P(None, "row", "col"), P()), check_vma=False
    )
```

```python
import functools
import math

import jax
import jax.numpy as jnp
import ml_dtypes
import numpy as np
from jax import lax
from jax.experimental import pallas as pl
from jax.experimental.pallas import tpu as pltpu
from jax.sharding import PartitionSpec as P

LANES = 128
SUBLANES = 8
GROUP = 2


def passed_along(value, axis, steps):
    count = lax.axis_size(axis)
    first, last = (max(0, -steps), min(count, count - steps))
    return lax.ppermute(value, axis, [(source, source + steps) for source in range(first, last)])


def bit_partners(axis):
    count = lax.axis_size(axis)
    return [(axis, 1 << power) for power in range(count.bit_length() - 1)]


def swapped(value, axis, bit):
    return lax.ppermute(value, axis, [(at, at ^ bit) for at in range(lax.axis_size(axis))])


def summed_over(value, axes):
    if any(lax.axis_size(axis) & (lax.axis_size(axis) - 1) for axis in axes):
        return lax.psum(value, axes)
    rounds = [pair for axis in axes for pair in bit_partners(axis)]
    shape = value.shape
    value = value.reshape(-1, shape[-1])
    split = []
    for axis, bit in rounds:
        half = value.shape[0] // 2
        if len(split) < 3 and half % SUBLANES == 0:
            upper = (lax.axis_index(axis) & bit) // bit
            kept = lax.dynamic_slice_in_dim(value, upper * half, half, 0)
            sent = lax.dynamic_slice_in_dim(value, (1 - upper) * half, half, 0)
            value = kept + swapped(sent, axis, bit)
            split.append((axis, bit, upper))
        else:
            value = value + swapped(value, axis, bit)
    for axis, bit, upper in reversed(split):
        other = swapped(value, axis, bit)
        first = jnp.where(upper == 0, value, other)
        second = jnp.where(upper == 0, other, value)
        value = jnp.concatenate([first, second], axis=0)
    return value.reshape(shape)


def halves_np(table):
    high = table.astype(ml_dtypes.bfloat16)
    low = (table - high.astype(np.float64)).astype(ml_dtypes.bfloat16)
    return high, low


def tables(size):
    index = np.arange(size)
    angle = (index[:, None] * index[None, :] % size) * (2.0 * math.pi / size)
    cosine, sine = np.cos(angle) / math.sqrt(size), np.sin(angle) / math.sqrt(size)
    left, right = [], []
    for table in (cosine, sine - cosine, cosine + sine):
        high, low = halves_np(table)
        left.append(np.concatenate([high, high, low], axis=1))
        right.append(np.concatenate([high, low, high], axis=0))
    return np.stack(left), np.stack(right)


def halves(value):
    high = value.astype(jnp.bfloat16)
    return high, (value - high.astype(jnp.float32)).astype(jnp.bfloat16)


def from_left(table, value):
    high, low = halves(value)
    return jnp.dot(table, jnp.concatenate([high, low, high], axis=0), preferred_element_type=jnp.float32)


def from_right(table, value):
    high, low = halves(value)
    return jnp.dot(jnp.concatenate([high, high, low], axis=1), table, preferred_element_type=jnp.float32)


def transform(real, imag, left, right, forward):
    for product, table in ((from_left, left), (from_right, right)):
        shared = product(table[0], real + imag)
        if forward:
            real, imag = shared + product(table[1], imag), shared - product(table[2], real)
        else:
            real, imag = shared - product(table[2], imag), shared + product(table[1], real)
    return real, imag


def kernel(dims, off, obj, below, right_top, right_low, corner, probe, amp, left_t, right_t,
           g_main, g_below, g_right_top, g_right_low, g_corner, probe_acc, ext, grad, sems):
    side, rows, cols = dims
    step = pl.program_id(0)

    def pieces(buf):
        return (
            buf.at[:, pl.ds(0, rows), pl.ds(0, cols)],
            buf.at[:, pl.ds(rows, side), pl.ds(0, cols)],
            buf.at[:, pl.ds(0, side), pl.ds(cols, side)],
            buf.at[:, pl.ds(side, rows - side), pl.ds(cols, side)],
            buf.at[:, pl.ds(rows, side), pl.ds(cols, side)],
        )

    @pl.when(step == 0)
    def _():
        copies = [
            pltpu.make_async_copy(source, place, sems.at[number])
            for number, (source, place) in enumerate(
                zip((obj, below, right_top, right_low, corner), pieces(ext))
            )
        ]
        for copy in copies:
            copy.start()
        grad[...] = jnp.zeros_like(grad)
        probe_acc[...] = jnp.zeros_like(probe_acc)
        for copy in copies:
            copy.wait()

    wide, tall = side + LANES, side + SUBLANES
    probe_r, probe_i = probe[0], probe[1]
    found = []
    for item in range(GROUP):
        top = off[0, 0, step * GROUP + item, 0]
        at = off[0, 0, step * GROUP + item, 1]
        base = pl.multiple_of(at // LANES * LANES, LANES)
        shift = at - base
        start = pl.multiple_of(top // SUBLANES * SUBLANES, SUBLANES)
        drop = top - start

        def view_of(part):
            window = ext[part, pl.ds(start, tall), pl.ds(base, wide)]
            window = pltpu.roll(window, lax.rem(wide - shift, wide), 1)[:, :side]
            return pltpu.roll(window, lax.rem(tall - drop, tall), 0)[:side]

        view_r, view_i = view_of(0), view_of(1)
        wave_r = probe_r * view_r - probe_i * view_i
        wave_i = probe_r * view_i + probe_i * view_r
        far_r, far_i = transform(wave_r, wave_i, left_t, right_t, True)
        keep = 1.0 - amp[item] * lax.rsqrt(jnp.maximum(far_r * far_r + far_i * far_i, 0.25))
        chi_r, chi_i = transform(far_r * keep, far_i * keep, left_t, right_t, False)
        found.append((start, drop, base, shift, view_r, view_i, chi_r, chi_i))
    for start, drop, base, shift, view_r, view_i, chi_r, chi_i in found:
        terms = (probe_r * chi_r + probe_i * chi_i, probe_r * chi_i - probe_i * chi_r)
        for part in range(2):
            term = jnp.concatenate([terms[part], jnp.zeros((SUBLANES, side), jnp.float32)], axis=0)
            term = pltpu.roll(term, drop, 0)
            term = jnp.concatenate([term, jnp.zeros((tall, LANES), jnp.float32)], axis=1)
            grad[part, pl.ds(start, tall), pl.ds(base, wide)] += pltpu.roll(term, shift, 1)
        probe_acc[0] += view_r * chi_r + view_i * chi_i
        probe_acc[1] += view_r * chi_i - view_i * chi_r

    @pl.when(step == pl.num_programs(0) - 1)
    def _():
        copies = [
            pltpu.make_async_copy(place, target, sems.at[number])
            for number, (place, target) in enumerate(
                zip(pieces(grad), (g_main, g_below, g_right_top, g_right_low, g_corner))
            )
        ]
        for copy in copies:
            copy.start()
        for copy in copies:
            copy.wait()


def all_positions(offsets, obj, below, right_top, right_low, corner, probe, amp):
    side, rows, cols = probe.shape[1], obj.shape[1], obj.shape[2]
    count = offsets.shape[2]
    left_t, right_t = tables(side)
    anywhere = pl.BlockSpec(memory_space=pl.ANY)
    whole = lambda *shape: pl.BlockSpec(shape, lambda step: (0,) * len(shape))
    f32 = jnp.float32
    shape = lambda *dims: jax.ShapeDtypeStruct(dims, f32)
    return pl.pallas_call(
        functools.partial(kernel, (side, rows, cols)),
        grid=(count // GROUP,),
        in_specs=[pl.BlockSpec(memory_space=pltpu.SMEM)] + [anywhere] * 5 + [
            whole(2, side, side),
            pl.BlockSpec((GROUP, side, side), lambda step: (step, 0, 0)),
            whole(*left_t.shape),
            whole(*right_t.shape),
        ],
        out_specs=[anywhere] * 5 + [whole(2, side, side)],
        out_shape=[
            shape(2, rows, cols),
            shape(2, side, cols),
            shape(2, side, side),
            shape(2, rows - side, side),
            shape(2, side, side),
            shape(2, side, side),
        ],
        scratch_shapes=[
            pltpu.VMEM((2, rows + side, cols + side), f32),
            pltpu.VMEM((2, rows + side, cols + side), f32),
            pltpu.SemaphoreType.DMA((5,)),
        ],
        compiler_params=pltpu.CompilerParams(vmem_limit_bytes=56 * 2**20),
        cost_estimate=pl.CostEstimate(
            flops=count * 36 * 2 * side**3, bytes_accessed=12 * 2**20, transcendentals=0
        ),
    )(offsets, obj, below, right_top, right_low, corner, probe, amp,
      jnp.asarray(left_t), jnp.asarray(right_t))


def shards(object_field, probe, amplitude, offsets):
    rows, cols = object_field.shape[1:]
    side = probe.shape[1]
    positions = offsets.shape[2]
    right_top = passed_along(object_field[:, :side, :side], "col", -1)
    right_low = passed_along(object_field[:, side:, :side], "col", -1)
    below = passed_along(object_field[:, :side, :], "row", -1)
    corner = passed_along(right_top, "row", -1)
    g_main, g_below, g_top, g_low, g_corner, probe_acc = all_positions(
        offsets, object_field, below, right_top, right_low, corner, probe,
        amplitude.reshape(amplitude.shape[2:]),
    )
    got_corner = passed_along(g_corner, "row", 1)
    got_low = passed_along(g_low, "col", 1)
    got_rows = passed_along(g_below, "row", 1)
    got_top = passed_along(g_top + got_corner, "col", 1)
    pad = lambda value, top: jnp.pad(
        value, ((0, 0), (top, rows - top - value.shape[1]), (0, cols - value.shape[2]))
    )
    object_grad = g_main + pad(got_rows, 0) + pad(got_top, 0) + pad(got_low, side)
    count = positions * lax.axis_size("row") * lax.axis_size("col")
    probe_total = summed_over(probe_acc, ("row", "col"))
    return (object_grad, probe_total / count)


def solution(mesh):
    placed = (
        P(None, "row", "col"),
        P(),
        P("row", "col", None, None, None),
        P("row", "col", None, None),
    )
    return jax.shard_map(
        shards, mesh=mesh, in_specs=placed, out_specs=(P(None, "row", "col"), P()), check_vma=False
    )
```

```python
import functools
import math

import jax
import jax.numpy as jnp
import ml_dtypes
import numpy as np
from jax import lax
from jax.experimental import pallas as pl
from jax.experimental.pallas import tpu as pltpu
from jax.sharding import PartitionSpec as P

LANES = 128
SUBLANES = 8
GROUP = 2


def passed_along(value, axis, steps):
    count = lax.axis_size(axis)
    first, last = (max(0, -steps), min(count, count - steps))
    return lax.ppermute(value, axis, [(source, source + steps) for source in range(first, last)])


def bit_partners(axis):
    count = lax.axis_size(axis)
    return [(axis, 1 << power) for power in range(count.bit_length() - 1)]


def swapped(value, axis, bit):
    return lax.ppermute(value, axis, [(at, at ^ bit) for at in range(lax.axis_size(axis))])


def summed_over(value, axes, corner, low, later):
    if any(lax.axis_size(axis) & (lax.axis_size(axis) - 1) for axis in axes):
        return lax.psum(value, axes), (low, *later(corner))
    rounds = [pair for axis in axes for pair in bit_partners(axis)]
    shape = value.shape
    value = value.reshape(-1, shape[-1])
    split = []
    for number, (axis, bit) in enumerate(rounds):
        if number == 1:
            value, corner = lax.optimization_barrier((value, corner))
        if number == 4:
            value, low = lax.optimization_barrier((value, low))
        half = value.shape[0] // 2
        if len(split) < 3 and half % SUBLANES == 0:
            upper = (lax.axis_index(axis) & bit) // bit
            kept = lax.dynamic_slice_in_dim(value, upper * half, half, 0)
            sent = lax.dynamic_slice_in_dim(value, (1 - upper) * half, half, 0)
            value = kept + swapped(sent, axis, bit)
            split.append((axis, bit, upper))
        else:
            value = value + swapped(value, axis, bit)
    beside = (low, *later(corner))
    for number, (axis, bit, upper) in enumerate(reversed(split)):
        if number == 1:
            value, beside = lax.optimization_barrier((value, beside))
        other = swapped(value, axis, bit)
        first = jnp.where(upper == 0, value, other)
        second = jnp.where(upper == 0, other, value)
        value = jnp.concatenate([first, second], axis=0)
    return value.reshape(shape), beside


def halves_np(table):
    high = table.astype(ml_dtypes.bfloat16)
    low = (table - high.astype(np.float64)).astype(ml_dtypes.bfloat16)
    return high, low


def tables(size):
    index = np.arange(size)
    angle = (index[:, None] * index[None, :] % size) * (2.0 * math.pi / size)
    cosine, sine = np.cos(angle) / math.sqrt(size), np.sin(angle) / math.sqrt(size)
    left, right = [], []
    for table in (cosine, sine - cosine, cosine + sine):
        high, low = halves_np(table)
        left.append(np.concatenate([high, high, low], axis=1))
        right.append(np.concatenate([high, low, high], axis=0))
    return np.stack(left), np.stack(right)


def halves(value):
    high = value.astype(jnp.bfloat16)
    return high, (value - high.astype(jnp.float32)).astype(jnp.bfloat16)


def from_left(table, value):
    high, low = halves(value)
    return jnp.dot(table, jnp.concatenate([high, low, high], axis=0), preferred_element_type=jnp.float32)


def from_right(table, value):
    high, low = halves(value)
    return jnp.dot(jnp.concatenate([high, high, low], axis=1), table, preferred_element_type=jnp.float32)


def transform(real, imag, left, right, forward):
    for product, table in ((from_left, left), (from_right, right)):
        shared = product(table[0], real + imag)
        if forward:
            real, imag = shared + product(table[1], imag), shared - product(table[2], real)
        else:
            real, imag = shared - product(table[2], imag), shared + product(table[1], real)
    return real, imag


def kernel(dims, off, obj, below, right_top, right_low, corner, probe, amp, left_t, right_t,
           g_main, g_below, g_right_top, g_right_low, g_corner, probe_acc, ext, grad, sems):
    side, rows, cols = dims
    step = pl.program_id(0)

    def pieces(buf):
        return (
            buf.at[:, pl.ds(0, rows), pl.ds(0, cols)],
            buf.at[:, pl.ds(rows, side), pl.ds(0, cols)],
            buf.at[:, pl.ds(0, side), pl.ds(cols, side)],
            buf.at[:, pl.ds(side, rows - side), pl.ds(cols, side)],
            buf.at[:, pl.ds(rows, side), pl.ds(cols, side)],
        )

    @pl.when(step == 0)
    def _():
        copies = [
            pltpu.make_async_copy(source, place, sems.at[number])
            for number, (source, place) in enumerate(
                zip((obj, below, right_top, right_low, corner), pieces(ext))
            )
        ]
        for copy in copies:
            copy.start()
        grad[...] = jnp.zeros_like(grad)
        probe_acc[...] = jnp.zeros_like(probe_acc)
        for copy in copies:
            copy.wait()

    wide, tall = side + LANES, side + SUBLANES
    probe_r, probe_i = probe[0], probe[1]
    found = []
    for item in range(GROUP):
        top = off[0, 0, step * GROUP + item, 0]
        at = off[0, 0, step * GROUP + item, 1]
        base = pl.multiple_of(at // LANES * LANES, LANES)
        shift = at - base
        start = pl.multiple_of(top // SUBLANES * SUBLANES, SUBLANES)
        drop = top - start

        def view_of(part):
            window = ext[part, pl.ds(start, tall), pl.ds(base, wide)]
            window = pltpu.roll(window, lax.rem(wide - shift, wide), 1)[:, :side]
            return pltpu.roll(window, lax.rem(tall - drop, tall), 0)[:side]

        view_r, view_i = view_of(0), view_of(1)
        wave_r = probe_r * view_r - probe_i * view_i
        wave_i = probe_r * view_i + probe_i * view_r
        far_r, far_i = transform(wave_r, wave_i, left_t, right_t, True)
        keep = 1.0 - amp[item] * lax.rsqrt(jnp.maximum(far_r * far_r + far_i * far_i, 0.25))
        chi_r, chi_i = transform(far_r * keep, far_i * keep, left_t, right_t, False)
        found.append((start, drop, base, shift, view_r, view_i, chi_r, chi_i))
    for start, drop, base, shift, view_r, view_i, chi_r, chi_i in found:
        terms = (probe_r * chi_r + probe_i * chi_i, probe_r * chi_i - probe_i * chi_r)
        for part in range(2):
            term = jnp.concatenate([terms[part], jnp.zeros((SUBLANES, side), jnp.float32)], axis=0)
            term = pltpu.roll(term, drop, 0)
            term = jnp.concatenate([term, jnp.zeros((tall, LANES), jnp.float32)], axis=1)
            grad[part, pl.ds(start, tall), pl.ds(base, wide)] += pltpu.roll(term, shift, 1)
        probe_acc[0] += view_r * chi_r + view_i * chi_i
        probe_acc[1] += view_r * chi_i - view_i * chi_r

    @pl.when(step == pl.num_programs(0) - 1)
    def _():
        copies = [
            pltpu.make_async_copy(place, target, sems.at[number])
            for number, (place, target) in enumerate(
                zip(pieces(grad), (g_main, g_below, g_right_top, g_right_low, g_corner))
            )
        ]
        for copy in copies:
            copy.start()
        for copy in copies:
            copy.wait()


def all_positions(offsets, obj, below, right_top, right_low, corner, probe, amp):
    side, rows, cols = probe.shape[1], obj.shape[1], obj.shape[2]
    count = offsets.shape[2]
    left_t, right_t = tables(side)
    anywhere = pl.BlockSpec(memory_space=pl.ANY)
    whole = lambda *shape: pl.BlockSpec(shape, lambda step: (0,) * len(shape))
    f32 = jnp.float32
    shape = lambda *dims: jax.ShapeDtypeStruct(dims, f32)
    return pl.pallas_call(
        functools.partial(kernel, (side, rows, cols)),
        grid=(count // GROUP,),
        in_specs=[pl.BlockSpec(memory_space=pltpu.SMEM)] + [anywhere] * 5 + [
            whole(2, side, side),
            pl.BlockSpec((GROUP, side, side), lambda step: (step, 0, 0)),
            whole(*left_t.shape),
            whole(*right_t.shape),
        ],
        out_specs=[anywhere] * 5 + [whole(2, side, side)],
        out_shape=[
            shape(2, rows, cols),
            shape(2, side, cols),
            shape(2, side, side),
            shape(2, rows - side, side),
            shape(2, side, side),
            shape(2, side, side),
        ],
        scratch_shapes=[
            pltpu.VMEM((2, rows + side, cols + side), f32),
            pltpu.VMEM((2, rows + side, cols + side), f32),
            pltpu.SemaphoreType.DMA((5,)),
        ],
        compiler_params=pltpu.CompilerParams(vmem_limit_bytes=56 * 2**20),
        cost_estimate=pl.CostEstimate(
            flops=count * 36 * 2 * side**3, bytes_accessed=12 * 2**20, transcendentals=0
        ),
    )(offsets, obj, below, right_top, right_low, corner, probe, amp,
      jnp.asarray(left_t), jnp.asarray(right_t))


def shards(object_field, probe, amplitude, offsets):
    rows, cols = object_field.shape[1:]
    side = probe.shape[1]
    positions = offsets.shape[2]
    right_top = passed_along(object_field[:, :side, :side], "col", -1)
    right_low = passed_along(object_field[:, side:, :side], "col", -1)
    below = passed_along(object_field[:, :side, :], "row", -1)
    corner = passed_along(right_top, "row", -1)
    g_main, g_below, g_top, g_low, g_corner, probe_acc = all_positions(
        offsets, object_field, below, right_top, right_low, corner, probe,
        amplitude.reshape(amplitude.shape[2:]),
    )
    got_corner = passed_along(g_corner, "row", 1)
    got_low = passed_along(g_low, "col", 1)
    later = lambda corner: (
        passed_along(g_below, "row", 1), passed_along(g_top + corner, "col", 1)
    )
    probe_total, (got_low, got_rows, got_top) = summed_over(
        probe_acc, ("row", "col"), got_corner, got_low, later
    )
    pad = lambda value, top: jnp.pad(
        value, ((0, 0), (top, rows - top - value.shape[1]), (0, cols - value.shape[2]))
    )
    object_grad = g_main + pad(got_rows, 0) + pad(got_top, 0) + pad(got_low, side)
    count = positions * lax.axis_size("row") * lax.axis_size("col")
    return (object_grad, probe_total / count)


def solution(mesh):
    placed = (
        P(None, "row", "col"),
        P(),
        P("row", "col", None, None, None),
        P("row", "col", None, None),
    )
    return jax.shard_map(
        shards, mesh=mesh, in_specs=placed, out_specs=(P(None, "row", "col"), P()), check_vma=False
    )
```

```python
import functools
import math

import jax
import jax.numpy as jnp
import ml_dtypes
import numpy as np
from jax import lax
from jax.experimental import pallas as pl
from jax.experimental.pallas import tpu as pltpu
from jax.sharding import PartitionSpec as P

LANES = 128
SUBLANES = 8
GROUP = 4


def passed_along(value, axis, steps):
    count = lax.axis_size(axis)
    first, last = (max(0, -steps), min(count, count - steps))
    return lax.ppermute(value, axis, [(source, source + steps) for source in range(first, last)])


def bit_partners(axis):
    count = lax.axis_size(axis)
    return [(axis, 1 << power) for power in range(count.bit_length() - 1)]


def swapped(value, axis, bit):
    return lax.ppermute(value, axis, [(at, at ^ bit) for at in range(lax.axis_size(axis))])


def summed_over(value, axes, corner, low, later):
    if any(lax.axis_size(axis) & (lax.axis_size(axis) - 1) for axis in axes):
        return lax.psum(value, axes), (low, *later(corner))
    rounds = [pair for axis in axes for pair in bit_partners(axis)]
    shape = value.shape
    value = value.reshape(-1, shape[-1])
    split = []
    for number, (axis, bit) in enumerate(rounds):
        if number == 1:
            value, corner = lax.optimization_barrier((value, corner))
        if number == 4:
            value, low = lax.optimization_barrier((value, low))
        half = value.shape[0] // 2
        if len(split) < 3 and half % SUBLANES == 0:
            upper = (lax.axis_index(axis) & bit) // bit
            kept = lax.dynamic_slice_in_dim(value, upper * half, half, 0)
            sent = lax.dynamic_slice_in_dim(value, (1 - upper) * half, half, 0)
            value = kept + swapped(sent, axis, bit)
            split.append((axis, bit, upper))
        else:
            value = value + swapped(value, axis, bit)
    beside = (low, *later(corner))
    for number, (axis, bit, upper) in enumerate(reversed(split)):
        if number == 1:
            value, beside = lax.optimization_barrier((value, beside))
        other = swapped(value, axis, bit)
        first = jnp.where(upper == 0, value, other)
        second = jnp.where(upper == 0, other, value)
        value = jnp.concatenate([first, second], axis=0)
    return value.reshape(shape), beside


def halves_np(table):
    high = table.astype(ml_dtypes.bfloat16)
    low = (table - high.astype(np.float64)).astype(ml_dtypes.bfloat16)
    return high, low


def tables(size):
    index = np.arange(size)
    angle = (index[:, None] * index[None, :] % size) * (2.0 * math.pi / size)
    cosine, sine = np.cos(angle) / math.sqrt(size), np.sin(angle) / math.sqrt(size)
    left, right = [], []
    for table in (cosine, sine - cosine, cosine + sine):
        high, low = halves_np(table)
        left.append(np.concatenate([high, high, low], axis=1))
        right.append(np.concatenate([high, low, high], axis=0))
    return np.stack(left), np.stack(right)


def halves(value):
    high = value.astype(jnp.bfloat16)
    return high, (value - high.astype(jnp.float32)).astype(jnp.bfloat16)


def from_left(table, value):
    high, low = halves(value)
    return jnp.dot(table, jnp.concatenate([high, low, high], axis=0), preferred_element_type=jnp.float32)


def from_right(table, value):
    high, low = halves(value)
    return jnp.dot(jnp.concatenate([high, high, low], axis=1), table, preferred_element_type=jnp.float32)


def transform(real, imag, left, right, forward):
    for product, table in ((from_left, left), (from_right, right)):
        shared = product(table[0], real + imag)
        if forward:
            real, imag = shared + product(table[1], imag), shared - product(table[2], real)
        else:
            real, imag = shared - product(table[2], imag), shared + product(table[1], real)
    return real, imag


def kernel(dims, off, obj, below, right_top, right_low, corner, probe, amp, left_t, right_t,
           g_main, g_below, g_right_top, g_right_low, g_corner, probe_acc, ext, grad, sems):
    side, rows, cols = dims
    step = pl.program_id(0)

    def pieces(buf):
        return (
            buf.at[:, pl.ds(0, rows), pl.ds(0, cols)],
            buf.at[:, pl.ds(rows, side), pl.ds(0, cols)],
            buf.at[:, pl.ds(0, side), pl.ds(cols, side)],
            buf.at[:, pl.ds(side, rows - side), pl.ds(cols, side)],
            buf.at[:, pl.ds(rows, side), pl.ds(cols, side)],
        )

    @pl.when(step == 0)
    def _():
        copies = [
            pltpu.make_async_copy(source, place, sems.at[number])
            for number, (source, place) in enumerate(
                zip((obj, below, right_top, right_low, corner), pieces(ext))
            )
        ]
        for copy in copies:
            copy.start()
        grad[...] = jnp.zeros_like(grad)
        probe_acc[...] = jnp.zeros_like(probe_acc)
        for copy in copies:
            copy.wait()

    wide, tall = side + LANES, side + SUBLANES
    probe_r, probe_i = probe[0], probe[1]
    found = []
    for item in range(GROUP):
        top = off[0, 0, step * GROUP + item, 0]
        at = off[0, 0, step * GROUP + item, 1]
        base = pl.multiple_of(at // LANES * LANES, LANES)
        shift = at - base
        start = pl.multiple_of(top // SUBLANES * SUBLANES, SUBLANES)
        drop = top - start

        def view_of(part):
            window = ext[part, pl.ds(start, tall), pl.ds(base, wide)]
            window = pltpu.roll(window, lax.rem(wide - shift, wide), 1)[:, :side]
            return pltpu.roll(window, lax.rem(tall - drop, tall), 0)[:side]

        view_r, view_i = view_of(0), view_of(1)
        wave_r = probe_r * view_r - probe_i * view_i
        wave_i = probe_r * view_i + probe_i * view_r
        far_r, far_i = transform(wave_r, wave_i, left_t, right_t, True)
        keep = 1.0 - amp[item] * lax.rsqrt(jnp.maximum(far_r * far_r + far_i * far_i, 0.25))
        chi_r, chi_i = transform(far_r * keep, far_i * keep, left_t, right_t, False)
        found.append((start, drop, base, shift, view_r, view_i, chi_r, chi_i))
    for start, drop, base, shift, view_r, view_i, chi_r, chi_i in found:
        terms = (probe_r * chi_r + probe_i * chi_i, probe_r * chi_i - probe_i * chi_r)
        for part in range(2):
            term = jnp.concatenate([terms[part], jnp.zeros((SUBLANES, side), jnp.float32)], axis=0)
            term = pltpu.roll(term, drop, 0)
            term = jnp.concatenate([term, jnp.zeros((tall, LANES), jnp.float32)], axis=1)
            grad[part, pl.ds(start, tall), pl.ds(base, wide)] += pltpu.roll(term, shift, 1)
        probe_acc[0] += view_r * chi_r + view_i * chi_i
        probe_acc[1] += view_r * chi_i - view_i * chi_r

    @pl.when(step == pl.num_programs(0) - 1)
    def _():
        copies = [
            pltpu.make_async_copy(place, target, sems.at[number])
            for number, (place, target) in enumerate(
                zip(pieces(grad), (g_main, g_below, g_right_top, g_right_low, g_corner))
            )
        ]
        for copy in copies:
            copy.start()
        for copy in copies:
            copy.wait()


def all_positions(offsets, obj, below, right_top, right_low, corner, probe, amp):
    side, rows, cols = probe.shape[1], obj.shape[1], obj.shape[2]
    count = offsets.shape[2]
    left_t, right_t = tables(side)
    anywhere = pl.BlockSpec(memory_space=pl.ANY)
    whole = lambda *shape: pl.BlockSpec(shape, lambda step: (0,) * len(shape))
    f32 = jnp.float32
    shape = lambda *dims: jax.ShapeDtypeStruct(dims, f32)
    return pl.pallas_call(
        functools.partial(kernel, (side, rows, cols)),
        grid=(count // GROUP,),
        in_specs=[pl.BlockSpec(memory_space=pltpu.SMEM)] + [anywhere] * 5 + [
            whole(2, side, side),
            pl.BlockSpec((GROUP, side, side), lambda step: (step, 0, 0)),
            whole(*left_t.shape),
            whole(*right_t.shape),
        ],
        out_specs=[anywhere] * 5 + [whole(2, side, side)],
        out_shape=[
            shape(2, rows, cols),
            shape(2, side, cols),
            shape(2, side, side),
            shape(2, rows - side, side),
            shape(2, side, side),
            shape(2, side, side),
        ],
        scratch_shapes=[
            pltpu.VMEM((2, rows + side, cols + side), f32),
            pltpu.VMEM((2, rows + side, cols + side), f32),
            pltpu.SemaphoreType.DMA((5,)),
        ],
        compiler_params=pltpu.CompilerParams(vmem_limit_bytes=56 * 2**20),
        cost_estimate=pl.CostEstimate(
            flops=count * 36 * 2 * side**3, bytes_accessed=12 * 2**20, transcendentals=0
        ),
    )(offsets, obj, below, right_top, right_low, corner, probe, amp,
      jnp.asarray(left_t), jnp.asarray(right_t))


def shards(object_field, probe, amplitude, offsets):
    rows, cols = object_field.shape[1:]
    side = probe.shape[1]
    positions = offsets.shape[2]
    right_top = passed_along(object_field[:, :side, :side], "col", -1)
    right_low = passed_along(object_field[:, side:, :side], "col", -1)
    below = passed_along(object_field[:, :side, :], "row", -1)
    corner = passed_along(right_top, "row", -1)
    g_main, g_below, g_top, g_low, g_corner, probe_acc = all_positions(
        offsets, object_field, below, right_top, right_low, corner, probe,
        amplitude.reshape(amplitude.shape[2:]),
    )
    got_corner = passed_along(g_corner, "row", 1)
    got_low = passed_along(g_low, "col", 1)
    later = lambda corner: (
        passed_along(g_below, "row", 1), passed_along(g_top + corner, "col", 1)
    )
    probe_total, (got_low, got_rows, got_top) = summed_over(
        probe_acc, ("row", "col"), got_corner, got_low, later
    )
    pad = lambda value, top: jnp.pad(
        value, ((0, 0), (top, rows - top - value.shape[1]), (0, cols - value.shape[2]))
    )
    object_grad = g_main + pad(got_rows, 0) + pad(got_top, 0) + pad(got_low, side)
    count = positions * lax.axis_size("row") * lax.axis_size("col")
    return (object_grad, probe_total / count)


def solution(mesh):
    placed = (
        P(None, "row", "col"),
        P(),
        P("row", "col", None, None, None),
        P("row", "col", None, None),
    )
    return jax.shard_map(
        shards, mesh=mesh, in_specs=placed, out_specs=(P(None, "row", "col"), P()), check_vma=False
    )
```
